32 devices in a mesh: px: 16 (over z, x, core), pz: 2 (over y).
Axes of the slice: x: 2, y: 2, z: 4, core: 2. Of those that a mesh axis runs over, the one named last changes fastest.
Arguments:
- scalar_field: float32 [768, 384, 384], P('px', 'pz'), may hold values from -6 to 6
- prev_tendency: float32 [768, 384, 384], P('px', 'pz'), may hold values from -3 to 3
- velocity_u: bfloat16 [768, 384, 384], P('px', 'pz'), may hold values from -6 to 6
- velocity_v: bfloat16 [768, 384, 384], P('px', 'pz'), may hold values from -1.5 to 1.5
- velocity_w: bfloat16 [768, 384, 384], P('px', 'pz'), may hold values from -3 to 3
Outputs:
- scalar_next: float32 [768, 384, 384], P('px', 'pz')
- tendency: float32 [768, 384, 384], P('px', 'pz')
The draws below stay inside these ranges and needn't reach their ends.
All inputs are finite; a program needn't handle non-finite values.
Results may differ from the reference program's by a relative error of at most 0.0003.
Values may be sent and summed in bfloat16 or wider, within the bound.
No kernel may reach another device: no remote copies, remote signals or barrier semaphores. Data moves between devices by JAX's collectives and lax.ppermute only.
A program may use at most 512 MiB of HBM per device.

```python
import jax
import jax.numpy as jnp
from jax import lax

NX = 768
NY = 384
NZ = 384


def levels(own_key, shape, shards, low, top_value):
    def one(dim, parts):
        steps = jax.random.uniform(jax.random.fold_in(jax.random.fold_in(own_key, 6), dim), (parts,), jnp.float32, low / len(shards), top_value / len(shards))
        return jnp.repeat(jnp.exp(steps), shape[dim] // parts).reshape((-1,) + (1,) * (len(shape) - dim - 1))

    level = one(*shards[0])
    for cut in shards[1:]:
        level = level * one(*cut)
    return level


def centred(own_key, dims, spread, most, shards=(), kind=jnp.bfloat16):
    values = spread * jax.random.normal(own_key, dims, jnp.float32)
    if shards:
        values = values * levels(own_key, dims, shards, -0.22, 0.18)
    return jnp.clip(values, -most, most).astype(kind)


def setup_inputs(seed: int = 0) -> dict:
    splits = jax.random.split(jax.random.key(seed), 6)
    return {
        "scalar_field": centred(splits[0], (NX, NY, NZ), 1.0, 6.0, ((0, 16), (1, 2)), jnp.float32),
        "prev_tendency": centred(splits[1], (NX, NY, NZ), 0.5, 3.0, ((0, 16), (1, 2)), jnp.float32),
        "velocity_u": centred(splits[2], (NX, NY, NZ), 1.0, 6.0, ((0, 16), (1, 2))),
        "velocity_v": centred(splits[3], (NX, NY, NZ), 0.25, 1.5, ((0, 16), (1, 2))),
        "velocity_w": centred(splits[4], (NX, NY, NZ), 0.5, 3.0, ((0, 16), (1, 2))),
    }


KAPPA = 1.0 / (550.0 * 0.71)
DT_STEP = 0.005
GAMMA_RK = 8.0 / 15.0
ZETA_RK = -17.0 / 60.0
LENGTH_X = 4.0 * 3.141592653589793
LENGTH_Z = 4.0 * 3.141592653589793 / 3.0


def wall_operator(points):
    intervals = points - 1
    row_index = jnp.arange(points, dtype=jnp.int32)
    row_grid = row_index[:, None]
    col_grid = row_index[None, :]
    node_angle = row_index.astype(jnp.float32) * (jnp.pi / intervals)
    node_values = jnp.cos(node_angle)
    half_step = jnp.pi / (2.0 * intervals)
    sum_angle = (row_grid + col_grid).astype(jnp.float32) * half_step
    differ = (row_grid - col_grid).astype(jnp.float32) * half_step
    node_gap = -2.0 * jnp.sin(sum_angle) * jnp.sin(differ)
    same_node = row_grid == col_grid
    safe_gap = jnp.where(same_node, jnp.float32(1.0), node_gap)
    interior = (row_index > 0) & (row_index < intervals)
    weight = jnp.where(interior, jnp.float32(1.0), jnp.float32(2.0))
    parity = (1 - 2 * ((row_grid + col_grid) % 2)).astype(jnp.float32)
    damping = jnp.square(jnp.sin(node_angle))
    off_diagonal = damping[:, None] * (weight[:, None] / weight[None, :]) * parity / safe_gap
    diagonal = jnp.where(interior, -0.5 * node_values, jnp.float32(0.0))
    full = jnp.where(same_node, diagonal[:, None] * jnp.ones_like(off_diagonal), off_diagonal)
    return jnp.where(interior[:, None], full, jnp.float32(0.0))


def spectral_pair(plane_field, along_axis, extent, length):
    spectrum = jnp.fft.rfft(plane_field, axis=along_axis)
    mode_index = jnp.arange(extent // 2 + 1, dtype=jnp.int32)
    wavenumber = mode_index.astype(jnp.float32) * (2.0 * jnp.pi / length)
    wavenumber = jnp.where(mode_index < extent // 3, wavenumber, jnp.float32(0.0))
    layout = [1, 1]
    layout[along_axis] = -1
    wavenumber = wavenumber.reshape(layout)
    first_deriv = jnp.fft.irfft(1j * wavenumber * spectrum, n=extent, axis=along_axis)
    second_deriv = jnp.fft.irfft(-(wavenumber * wavenumber) * spectrum, n=extent, axis=along_axis)
    return first_deriv.real.astype(jnp.float32), second_deriv.real.astype(jnp.float32)


def reference(scalar_field, prev_tendency, velocity_u, velocity_v, velocity_w):
    wall_matrix = wall_operator(NY)

    def one_plane(plane_index):
        plane_field = lax.dynamic_index_in_dim(scalar_field, plane_index, 1, keepdims=False)
        wall_row = lax.dynamic_index_in_dim(wall_matrix, plane_index, 0, keepdims=False)
        wall_slope = jnp.tensordot(wall_row, scalar_field, axes=(0, 1), precision=lax.Precision.HIGHEST)
        x_first, x_second = spectral_pair(plane_field, 0, NX, LENGTH_X)
        z_first, z_second = spectral_pair(plane_field, 1, NZ, LENGTH_Z)
        plane_u = lax.dynamic_index_in_dim(velocity_u, plane_index, 1, keepdims=False).astype(jnp.float32)
        plane_v = lax.dynamic_index_in_dim(velocity_v, plane_index, 1, keepdims=False).astype(jnp.float32)
        plane_w = lax.dynamic_index_in_dim(velocity_w, plane_index, 1, keepdims=False).astype(jnp.float32)
        plane_prev = lax.dynamic_index_in_dim(prev_tendency, plane_index, 1, keepdims=False)
        forcing = plane_u * x_first + plane_v * wall_slope + plane_w * z_first + KAPPA * (x_second + z_second)
        plane_tend = DT_STEP * forcing
        plane_next = plane_field + GAMMA_RK * plane_tend + ZETA_RK * plane_prev
        return plane_next, plane_tend

    stacked_next, stacked_tend = lax.map(one_plane, jnp.arange(NY, dtype=jnp.int32))
    return jnp.transpose(stacked_next, (1, 0, 2)), jnp.transpose(stacked_tend, (1, 0, 2))
```

```python
import functools

import jax
import jax.numpy as jnp
import ml_dtypes
import numpy as np
from jax import lax
from jax.experimental import pallas as pl
from jax.experimental.pallas import tpu as pltpu
from jax.sharding import PartitionSpec as P

KAPPA = 1.0 / (550.0 * 0.71)
DT_STEP = 0.005
GAMMA_RK = 8.0 / 15.0
ZETA_RK = -17.0 / 60.0
LENGTH_X = 4.0 * 3.141592653589793
LENGTH_Z = 4.0 * 3.141592653589793 / 3.0

F32 = jnp.float32
BF16 = jnp.bfloat16
VMEM = 56 << 20

SCALAR_BOUND = 6.0
VELOCITY_BOUND = 6.0
CODE_TOP = 120.0
SCALAR_RATE = CODE_TOP / (0.5 * SCALAR_BOUND)
STREAM_UNIT = 8.0
LOG2E = 1.4426950408889634


def wall_table(points):
    j = np.arange(points)
    angle = np.pi * j / (points - 1)
    node = np.cos(angle)
    weight = np.where((j == 0) | (j == points - 1), 2.0, 1.0)
    half = 0.5 * np.pi / (points - 1)
    gap = -2.0 * np.sin((j[:, None] + j[None, :]) * half) * np.sin((j[:, None] - j[None, :]) * half)
    gap[j, j] = 1.0
    parity = 1.0 - 2.0 * ((j[:, None] + j[None, :]) % 2)
    table = (np.sin(angle) ** 2)[:, None] * (weight[:, None] / weight[None, :]) * parity / gap
    table[j, j] = -0.5 * node
    table[0, :] = 0.0
    table[-1, :] = 0.0
    return table


def fourier_kernels(extent, length):
    mode = np.arange(extent // 3)
    wave = mode * (2.0 * np.pi / length)
    phase = 2.0 * np.pi * (np.outer(np.arange(extent), mode) % extent) / extent
    first = -(2.0 / extent) * (np.sin(phase) @ wave)
    second = -(2.0 * KAPPA / extent) * (np.cos(phase) @ (wave * wave))
    return first, second


def circulant(column):
    n = column.shape[0]
    i = np.arange(n)
    return column[(i[:, None] - i[None, :]) % n]


def two_terms(table):
    table = np.asarray(table, np.float32)
    high = table.astype(ml_dtypes.bfloat16)
    low = (table - high.astype(np.float32)).astype(ml_dtypes.bfloat16)
    return np.stack([high, low])


def encode_scalar(x):
    size = jnp.exp2(SCALAR_RATE * jnp.abs(x) - CODE_TOP)
    return jnp.where(x < 0, -size, size)


def decode_scalar(b):
    size = (jnp.log(jnp.abs(b)) * LOG2E + CODE_TOP) * (1.0 / SCALAR_RATE)
    return jnp.where(b < 0, -size, size)


def encode_stream(x, rate):
    size = jnp.exp2((rate * LOG2E) * jnp.log(1.0 + jnp.abs(x) * (1.0 / STREAM_UNIT)) - CODE_TOP)
    return jnp.where(x < 0, -size, size)


def decode_stream(b, rate):
    size = STREAM_UNIT * (jnp.exp2((jnp.log(jnp.abs(b)) * LOG2E + CODE_TOP) * (1.0 / rate)) - 1.0)
    return jnp.where(b < 0, -size, size)


def split(x):
    high = x.astype(BF16)
    return high, (x - high.astype(F32)).astype(BF16)


def dot(a, b):
    return jnp.dot(a, b, preferred_element_type=F32)


def dot3(a_high, a_low, b_high, b_low):
    return dot(a_high, b_high) + dot(a_high, b_low) + dot(a_low, b_high)


def params(**kw):
    return pltpu.CompilerParams(vmem_limit_bytes=VMEM, **kw)


def cost(flops, moved):
    return pl.CostEstimate(flops=int(flops), bytes_accessed=int(moved), transcendentals=0)


STEP = 16


def pack_kernel(f_ref, u_ref, g_ref, w_ref):
    code = encode_scalar(f_ref[...])
    g_ref[...] = jnp.swapaxes(code, 0, 1).astype(BF16).reshape(g_ref.shape)
    u = jnp.swapaxes(u_ref[...].astype(F32), 0, 1)
    w_ref[...] = u.astype(BF16).reshape(w_ref.shape)


def pack(f, u, first_row, rows, shares):
    nx, ny, nz = f.shape
    each = rows // shares
    per = STEP // each
    out = jax.ShapeDtypeStruct((shares, each, nx, nz), BF16)
    base = first_row // STEP
    return pl.pallas_call(
        pack_kernel,
        grid=(rows // STEP,),
        in_specs=[pl.BlockSpec((nx, STEP, nz), lambda i: (0, base + i, 0))] * 2,
        out_specs=[pl.BlockSpec((per, each, nx, nz), lambda i: (i, 0, 0, 0))] * 2,
        out_shape=[out, out],
        compiler_params=params(),
        cost_estimate=cost(0, rows * nx * nz * 10),
    )(f, u)


def code_kernel(f_ref, h_ref):
    h_ref[...] = encode_scalar(f_ref[...]).astype(BF16)


def code(f, first, planes):
    _, ny, nz = f.shape
    step = 4
    base = first // step
    return pl.pallas_call(
        code_kernel,
        grid=(planes // step,),
        in_specs=[pl.BlockSpec((step, ny, nz), lambda i: (base + i, 0, 0))],
        out_specs=pl.BlockSpec((step, ny, nz), lambda i: (i, 0, 0)),
        out_shape=jax.ShapeDtypeStruct((planes, ny, nz), BF16),
        compiler_params=params(),
        cost_estimate=cost(0, planes * ny * nz * 6),
    )(f)


def stream_kernel(n_in, n_out, rate, table_ref, *refs):
    f_refs, u_refs, s_refs = refs[:n_in], refs[n_in:n_in + n_out], refs[n_in + n_out:]
    rows = refs[0].shape[1]
    nz = refs[0].shape[3]
    columns = []
    for k in range(rows):
        blocks = [r[:, k].astype(F32).reshape(-1, nz) for r in f_refs]
        columns.append(jnp.concatenate(blocks, axis=0) if n_in > 1 else blocks[0])
    field = decode_scalar(jnp.concatenate(columns, axis=1))
    high, low = split(field)
    start = 0
    for o in range(n_out):
        parts, nx = u_refs[o].shape[0], u_refs[o].shape[2]
        bunch = 4
        for s in range(0, parts, bunch):
            tall = bunch * nx
            pair = []
            for which in range(2):
                t_high = table_ref[0, which, pl.ds(start, tall), :]
                t_low = table_ref[1, which, pl.ds(start, tall), :]
                pair.append(dot3(t_high, t_low, high, low))
            for k in range(rows):
                cols = slice(k * nz, (k + 1) * nz)
                u = u_refs[o][s:s + bunch, k].astype(F32).reshape(tall, nz)
                value = u * pair[0][:, cols] + pair[1][:, cols]
                coded = encode_stream(value, rate).astype(BF16)
                s_refs[o][s:s + bunch, k] = coded.reshape(bunch, nx, nz)
            start += tall


def stream(table, fields, speeds, rate):
    parts, rows, nx, nz = fields[0].shape
    n_in, n_out = len(fields), len(speeds)
    step = 2 if rows % 2 == 0 else 1
    block = pl.BlockSpec((parts, step, nx, nz), lambda i: (0, i, 0, 0))
    whole = pl.BlockSpec(table.shape, lambda i: (0, 0, 0, 0), pipeline_mode=pl.Buffered(1))
    points = table.shape[2] * table.shape[3]
    moved = 2 * (n_in + 2 * n_out) * parts * rows * nx * nz
    return pl.pallas_call(
        functools.partial(stream_kernel, n_in, n_out, rate),
        grid=(rows // step,),
        in_specs=[whole] + [block] * (n_in + n_out),
        out_specs=[block] * n_out,
        out_shape=[jax.ShapeDtypeStruct(fields[0].shape, BF16)] * n_out,
        compiler_params=params(),
        cost_estimate=cost(12 * points * rows * nz, moved),
    )(table, *fields, *speeds)


def local_kernel(wall_ref, span_ref, f_ref, h_ref, v_ref, w_ref, p_ref, *refs):
    next_ref, tend_ref = refs[-2:]
    planes, ny, nz = f_ref.shape
    own = f_ref[...]
    other = decode_scalar(h_ref[...].astype(F32))
    own_high, own_low = split(own)
    other_high, other_low = split(other)

    def stack(a, b):
        return jnp.concatenate(
            [jnp.concatenate([a[x], b[x]], axis=0) for x in range(planes)], axis=1
        )

    y_high, y_low = stack(own_high, other_high), stack(own_low, other_low)
    slope = dot3(wall_ref[0], wall_ref[1], y_high, y_low)
    z_high, z_low = own_high.reshape(-1, nz), own_low.reshape(-1, nz)
    span = dot3(z_high, z_low, span_ref[0], span_ref[1])
    for x in range(planes):
        rows = slice(x * ny, (x + 1) * ny)
        forcing = (
            v_ref[x].astype(F32) * slope[:, x * nz:(x + 1) * nz]
            + w_ref[x].astype(F32) * span[rows, :nz]
            + span[rows, nz:]
        )
        tendency = DT_STEP * forcing
        tend_ref[x] = tendency
        next_ref[x] = own[x] + GAMMA_RK * tendency + ZETA_RK * p_ref[x]


def local(wall, span, f, h, v, w, prev, first, held):
    nx, ny, nz = f.shape
    planes = h.shape[0]
    step = 2
    base = first // step
    block = pl.BlockSpec((step, ny, nz), lambda i: (base + i, 0, 0))
    table = lambda t: pl.BlockSpec(t.shape, lambda i: (0, 0, 0), pipeline_mode=pl.Buffered(1))
    out = jax.ShapeDtypeStruct(f.shape, F32)
    keep = pl.BlockSpec(memory_space=pl.ANY)
    return pl.pallas_call(
        local_kernel,
        grid=(planes // step,),
        in_specs=[table(wall), table(span), block,
                  pl.BlockSpec((step, ny, nz), lambda i: (i, 0, 0)), block, block, block]
        + [keep] * len(held),
        out_specs=[block, block],
        out_shape=[out, out],
        input_output_aliases={7 + k: k for k in range(len(held))},
        compiler_params=params(),
        cost_estimate=cost(6 * planes * ny * nz * (2 * ny + 2 * nz), planes * ny * nz * 22),
    )(wall, span, f, h, v, w, prev, *held)


def merge_kernel(rate, s_ref, next_ref, tend_ref, next_out, tend_out):
    nx, step, nz = next_ref.shape
    coded = jnp.swapaxes(s_ref[...].astype(F32).reshape(step, nx, nz), 0, 1)
    add = DT_STEP * decode_stream(coded, rate)
    tend_out[...] = tend_ref[...] + add
    next_out[...] = next_ref[...] + GAMMA_RK * add


def merge(s, held, first_row, rate):
    nx, ny, nz = held[0].shape
    shares, each = s.shape[:2]
    per = STEP // each
    base = first_row // STEP
    block = pl.BlockSpec((nx, STEP, nz), lambda i: (0, base + i, 0))
    out = jax.ShapeDtypeStruct(held[0].shape, F32)
    return pl.pallas_call(
        functools.partial(merge_kernel, rate),
        grid=(shares * each // STEP,),
        in_specs=[pl.BlockSpec((per, each, nx, nz), lambda i: (i, 0, 0, 0)), block, block],
        out_specs=[block, block],
        out_shape=[out, out],
        input_output_aliases={1: 0, 2: 1},
        compiler_params=params(),
        cost_estimate=cost(0, shares * each * nx * nz * 18),
    )(s, *held)


CHUNKS = (32,) * 6
PIECES = 4
PLAIN = False


def body(px, pz, f, prev, u, v, w):
    nx, ny, nz = f.shape
    nxg = nx * px
    first, second = fourier_kernels(nxg, LENGTH_X)
    rate_bound = VELOCITY_BOUND * SCALAR_BOUND * np.abs(first).sum() + SCALAR_BOUND * np.abs(second).sum()
    rate = float(2 * CODE_TOP / np.log2(1.0 + 1.02 * rate_bound / STREAM_UNIT))
    k_first, k_second = circulant(first), circulant(second)
    z_first, z_second = (circulant(c) for c in fourier_kernels(nz, LENGTH_Z))
    span = jnp.asarray(two_terms(np.concatenate([z_first.T, z_second.T], axis=1)))
    walls = wall_table(ny * pz)
    mine = lax.axis_index("pz")
    wall_all = []
    for y in range(pz):
        rows = walls[y * ny:(y + 1) * ny]
        own = rows[:, y * ny:(y + 1) * ny]
        other = rows[:, (1 - y) * ny:(2 - y) * ny]
        wall_all.append(two_terms(np.concatenate([own, other], axis=1)))
    wall = lax.dynamic_index_in_dim(jnp.asarray(np.stack(wall_all)), mine, 0, keepdims=False)

    planes = nx // PIECES
    theirs = []
    for p in range(PIECES):
        theirs.append(lax.ppermute(code(f, p * planes, planes), "pz", [(0, 1), (1, 0)]))

    starts = np.concatenate([[0], np.cumsum(CHUNKS)])[:-1]
    streams = []
    if PLAIN:
        table = jnp.asarray(np.stack([two_terms(k_first), two_terms(k_second)], axis=1))
        for at, rows in zip(starts, CHUNKS):
            g, ut = pack(f, u, int(at), rows, px)
            g = lax.all_to_all(g, "px", 0, 0, tiled=True)
            ut = lax.all_to_all(ut, "px", 0, 0, tiled=True)
            (s,) = stream(table, [g], [ut], rate)
            streams.append(lax.all_to_all(s, "px", 0, 0, tiled=True))
    else:
        ring = px // 4
        quarter = nx * ring
        variants = []
        for order in ((1, 0, 2, 3), (2, 3, 1, 0)):
            pick = lambda m: np.concatenate(
                [np.concatenate([m[o * quarter:(o + 1) * quarter, q * quarter:(q + 1) * quarter] for q in order], axis=1)
                 for o in order[:2]], axis=0)
            variants.append(np.stack([two_terms(pick(k_first)), two_terms(pick(k_second))], axis=1))
        level = lax.axis_index("px") // ring
        table = lax.dynamic_index_in_dim(jnp.asarray(np.stack(variants)), level // 2, 0, keepdims=False)
        outer = (level == 0) | (level == 3)
        groups = [[l * ring + r for r in range(ring)] for l in range(4)]
        hop = lambda pairs: [(a * ring + r, b * ring + r) for a, b in pairs for r in range(ring)]
        inward, across, outward = hop([(0, 1), (3, 2)]), hop([(1, 2), (2, 1)]), hop([(1, 0), (2, 3)])
        for at, rows in zip(starts, CHUNKS):
            g, ut = pack(f, u, int(at), rows, ring)
            g = lax.all_to_all(g, "px", 0, 0, axis_index_groups=groups, tiled=True)
            ut = lax.all_to_all(ut, "px", 0, 0, axis_index_groups=groups, tiled=True)
            near = lax.ppermute(g, "px", inward)
            far = lax.ppermute(g, "px", across)
            near_u = lax.ppermute(ut, "px", inward)
            far_near = lax.ppermute(near, "px", across)
            s_own, s_near = stream(table, [g, near, far, far_near], [ut, near_u], rate)
            got = lax.ppermute(s_near, "px", outward)
            s = jnp.where(outer, got, s_own)
            streams.append(lax.all_to_all(s, "px", 0, 0, axis_index_groups=groups, tiled=True))

    held = ()
    for p in range(PIECES):
        held = tuple(local(wall, span, f, theirs[p], v, w, prev, p * planes, held))
    for at, s in zip(starts, streams):
        held = tuple(merge(s, held, int(at), rate))
    return held


def plain_wall(points):
    return jnp.asarray(wall_table(points), F32)


def plain_body(scalar_field, prev_tendency, velocity_u, velocity_v, velocity_w):
    highest = lax.Precision.HIGHEST
    z_tables = [circulant(c) for c in fourier_kernels(scalar_field.shape[2], LENGTH_Z)]
    z_first, z_diffusion = (
        jnp.einsum("ij,abj->abi", jnp.asarray(t, F32), scalar_field, precision=highest) for t in z_tables
    )
    normal = lax.all_to_all(scalar_field, "pz", split_axis=2, concat_axis=1, tiled=True)
    slope = jnp.einsum("ij,ajb->aib", plain_wall(normal.shape[1]), normal, precision=highest)
    slope = lax.all_to_all(slope, "pz", split_axis=1, concat_axis=2, tiled=True)
    pencil = lax.all_to_all(scalar_field, "px", split_axis=2, concat_axis=0, tiled=True)
    x_tables = [circulant(c) for c in fourier_kernels(pencil.shape[0], LENGTH_X)]
    x_first, x_diffusion = (
        lax.all_to_all(
            jnp.einsum("ij,jab->iab", jnp.asarray(t, F32), pencil, precision=highest),
            "px", split_axis=0, concat_axis=2, tiled=True,
        )
        for t in x_tables
    )
    forcing = (
        velocity_u.astype(F32) * x_first
        + x_diffusion
        + velocity_v.astype(F32) * slope
        + velocity_w.astype(F32) * z_first
        + z_diffusion
    )
    tendency = DT_STEP * forcing
    return scalar_field + GAMMA_RK * tendency + ZETA_RK * prev_tendency, tendency


def fits(px, pz, shape):
    nx, ny, nz = shape
    return px == 16 and pz == 2 and nx % 16 == 0 and ny == sum(CHUNKS) and nz % 128 == 0


def whole_body(px, pz, *arrays):
    if fits(px, pz, arrays[0].shape):
        return body(px, pz, *arrays)
    return plain_body(*arrays)


def solution(mesh):
    px, pz = mesh.shape["px"], mesh.shape["pz"]
    spec = P("px", "pz", None)
    return jax.shard_map(
        functools.partial(whole_body, px, pz),
        mesh=mesh,
        in_specs=(spec,) * 5,
        out_specs=(spec, spec),
        check_vma=False,
    )
```

```python
import functools

import jax
import jax.numpy as jnp
import ml_dtypes
import numpy as np
from jax import lax
from jax.experimental import pallas as pl
from jax.experimental.pallas import tpu as pltpu
from jax.sharding import PartitionSpec as P

KAPPA = 1.0 / (550.0 * 0.71)
DT_STEP = 0.005
GAMMA_RK = 8.0 / 15.0
ZETA_RK = -17.0 / 60.0
LENGTH_X = 4.0 * 3.141592653589793
LENGTH_Z = 4.0 * 3.141592653589793 / 3.0

F32 = jnp.float32
BF16 = jnp.bfloat16
VMEM = 56 << 20

SCALAR_BOUND = 6.0
VELOCITY_BOUND = 6.0
CODE_TOP = 120.0
SCALAR_RATE = CODE_TOP / (0.5 * SCALAR_BOUND)
STREAM_UNIT = 8.0
LOG2E = 1.4426950408889634


def wall_table(points):
    j = np.arange(points)
    angle = np.pi * j / (points - 1)
    node = np.cos(angle)
    weight = np.where((j == 0) | (j == points - 1), 2.0, 1.0)
    half = 0.5 * np.pi / (points - 1)
    gap = -2.0 * np.sin((j[:, None] + j[None, :]) * half) * np.sin((j[:, None] - j[None, :]) * half)
    gap[j, j] = 1.0
    parity = 1.0 - 2.0 * ((j[:, None] + j[None, :]) % 2)
    table = (np.sin(angle) ** 2)[:, None] * (weight[:, None] / weight[None, :]) * parity / gap
    table[j, j] = -0.5 * node
    table[0, :] = 0.0
    table[-1, :] = 0.0
    return table


def fourier_kernels(extent, length):
    mode = np.arange(extent // 3)
    wave = mode * (2.0 * np.pi / length)
    phase = 2.0 * np.pi * (np.outer(np.arange(extent), mode) % extent) / extent
    first = -(2.0 / extent) * (np.sin(phase) @ wave)
    second = -(2.0 * KAPPA / extent) * (np.cos(phase) @ (wave * wave))
    return first, second


def circulant(column):
    n = column.shape[0]
    i = np.arange(n)
    return column[(i[:, None] - i[None, :]) % n]


def two_terms(table):
    table = np.asarray(table, np.float32)
    high = table.astype(ml_dtypes.bfloat16)
    low = (table - high.astype(np.float32)).astype(ml_dtypes.bfloat16)
    return np.stack([high, low])


def encode_scalar(x):
    size = jnp.exp2(SCALAR_RATE * jnp.abs(x) - CODE_TOP)
    return jnp.where(x < 0, -size, size)


def decode_scalar(b):
    size = (jnp.log(jnp.abs(b)) * LOG2E + CODE_TOP) * (1.0 / SCALAR_RATE)
    return jnp.where(b < 0, -size, size)


def encode_stream(x, rate):
    size = jnp.exp2((rate * LOG2E) * jnp.log(1.0 + jnp.abs(x) * (1.0 / STREAM_UNIT)) - CODE_TOP)
    return jnp.where(x < 0, -size, size)


def decode_stream(b, rate):
    size = STREAM_UNIT * (jnp.exp2((jnp.log(jnp.abs(b)) * LOG2E + CODE_TOP) * (1.0 / rate)) - 1.0)
    return jnp.where(b < 0, -size, size)


def split(x):
    high = x.astype(BF16)
    return high, (x - high.astype(F32)).astype(BF16)


def dot(a, b):
    return jnp.dot(a, b, preferred_element_type=F32)


def dot3(a_high, a_low, b_high, b_low):
    return dot(a_high, b_high) + dot(a_high, b_low) + dot(a_low, b_high)


def params(**kw):
    return pltpu.CompilerParams(vmem_limit_bytes=VMEM, **kw)


COST = 1.0


def cost(flops, moved):
    return pl.CostEstimate(flops=int(COST * flops), bytes_accessed=int(COST * moved), transcendentals=0)


def launch(kernel, operands, in_specs, after, **kw):
    count, extra = len(operands), len(after)

    def run(*refs):
        kernel(*refs[:count], *refs[count + extra:])

    return pl.pallas_call(
        run,
        in_specs=list(in_specs) + [pl.BlockSpec(memory_space=pl.ANY)] * extra,
        **kw,
    )(*operands, *after)


STEP = 16
MARK = jax.ShapeDtypeStruct((8, 128), F32)
MARK_BLOCK = pl.BlockSpec((8, 128), lambda i: (0, 0))


def pack_kernel(f_ref, u_ref, g_ref, w_ref):
    code = encode_scalar(f_ref[...])
    g_ref[...] = jnp.swapaxes(code, 0, 1).astype(BF16).reshape(g_ref.shape)
    u = jnp.swapaxes(u_ref[...].astype(F32), 0, 1)
    w_ref[...] = u.astype(BF16).reshape(w_ref.shape)


def pack(f, u, first_row, rows, shares, after):
    nx, ny, nz = f.shape
    each = rows // shares
    per = STEP // each
    out = jax.ShapeDtypeStruct((shares, each, nx, nz), BF16)
    base = first_row // STEP
    return launch(
        pack_kernel,
        (f, u),
        [pl.BlockSpec((nx, STEP, nz), lambda i: (0, base + i, 0))] * 2,
        after,
        grid=(rows // STEP,),
        out_specs=[pl.BlockSpec((per, each, nx, nz), lambda i: (i, 0, 0, 0))] * 2,
        out_shape=[out, out],
        compiler_params=params(),
        cost_estimate=cost(0, rows * nx * nz * 10),
    )


def code_kernel(f_ref, h_ref):
    h_ref[...] = encode_scalar(f_ref[...]).astype(BF16)


def code(f, first, planes, after):
    _, ny, nz = f.shape
    step = 4
    base = first // step
    return launch(
        code_kernel,
        (f,),
        [pl.BlockSpec((step, ny, nz), lambda i: (base + i, 0, 0))],
        after,
        grid=(planes // step,),
        out_specs=pl.BlockSpec((step, ny, nz), lambda i: (i, 0, 0)),
        out_shape=jax.ShapeDtypeStruct((planes, ny, nz), BF16),
        compiler_params=params(),
        cost_estimate=cost(0, planes * ny * nz * 6),
    )


def stream_kernel(n_in, n_out, rate, table_ref, *refs):
    f_refs, u_refs, s_refs = refs[:n_in], refs[n_in:n_in + n_out], refs[n_in + n_out:]
    rows = refs[0].shape[1]
    nz = refs[0].shape[3]
    columns = []
    for k in range(rows):
        blocks = [r[:, k].astype(F32).reshape(-1, nz) for r in f_refs]
        columns.append(jnp.concatenate(blocks, axis=0) if n_in > 1 else blocks[0])
    field = decode_scalar(jnp.concatenate(columns, axis=1))
    high, low = split(field)
    start = 0
    for o in range(n_out):
        parts, nx = u_refs[o].shape[0], u_refs[o].shape[2]
        bunch = 4
        for s in range(0, parts, bunch):
            tall = bunch * nx
            pair = []
            for which in range(2):
                t_high = table_ref[0, which, pl.ds(start, tall), :]
                t_low = table_ref[1, which, pl.ds(start, tall), :]
                pair.append(dot3(t_high, t_low, high, low))
            for k in range(rows):
                cols = slice(k * nz, (k + 1) * nz)
                u = u_refs[o][s:s + bunch, k].astype(F32).reshape(tall, nz)
                value = u * pair[0][:, cols] + pair[1][:, cols]
                coded = encode_stream(value, rate).astype(BF16)
                s_refs[o][s:s + bunch, k] = coded.reshape(bunch, nx, nz)
            start += tall


def stream(table, fields, speeds, rate, after):
    parts, rows, nx, nz = fields[0].shape
    n_in, n_out = len(fields), len(speeds)
    step = 2 if rows % 2 == 0 else 1
    block = pl.BlockSpec((parts, step, nx, nz), lambda i: (0, i, 0, 0))
    whole = pl.BlockSpec(table.shape, lambda i: (0, 0, 0, 0), pipeline_mode=pl.Buffered(1))
    points = table.shape[2] * table.shape[3]
    moved = 2 * (n_in + 2 * n_out) * parts * rows * nx * nz
    return launch(
        functools.partial(stream_kernel, n_in, n_out, rate),
        (table, *fields, *speeds),
        [whole] + [block] * (n_in + n_out),
        after,
        grid=(rows // step,),
        out_specs=[block] * n_out,
        out_shape=[jax.ShapeDtypeStruct(fields[0].shape, BF16)] * n_out,
        compiler_params=params(),
        cost_estimate=cost(12 * points * rows * nz, moved),
    )


def local_kernel(wall_ref, span_ref, f_ref, h_ref, v_ref, w_ref, p_ref, *refs):
    next_ref, tend_ref, mark_ref = refs[-3:]
    mark_ref[...] = jnp.zeros_like(mark_ref)
    planes, ny, nz = f_ref.shape
    own = f_ref[...]
    other = decode_scalar(h_ref[...].astype(F32))
    own_high, own_low = split(own)
    other_high, other_low = split(other)

    def stack(a, b):
        return jnp.concatenate(
            [jnp.concatenate([a[x], b[x]], axis=0) for x in range(planes)], axis=1
        )

    y_high, y_low = stack(own_high, other_high), stack(own_low, other_low)
    slope = dot3(wall_ref[0], wall_ref[1], y_high, y_low)
    z_high, z_low = own_high.reshape(-1, nz), own_low.reshape(-1, nz)
    span = dot3(z_high, z_low, span_ref[0], span_ref[1])
    for x in range(planes):
        rows = slice(x * ny, (x + 1) * ny)
        forcing = (
            v_ref[x].astype(F32) * slope[:, x * nz:(x + 1) * nz]
            + w_ref[x].astype(F32) * span[rows, :nz]
            + span[rows, nz:]
        )
        tendency = DT_STEP * forcing
        tend_ref[x] = tendency
        next_ref[x] = own[x] + GAMMA_RK * tendency + ZETA_RK * p_ref[x]


def local(wall, span, f, h, v, w, prev, first, held, after):
    nx, ny, nz = f.shape
    planes = h.shape[0]
    step = 2
    base = first // step
    block = pl.BlockSpec((step, ny, nz), lambda i: (base + i, 0, 0))
    table = lambda t: pl.BlockSpec(t.shape, lambda i: (0, 0, 0), pipeline_mode=pl.Buffered(1))
    out = jax.ShapeDtypeStruct(f.shape, F32)
    keep = pl.BlockSpec(memory_space=pl.ANY)
    return launch(
        local_kernel,
        (wall, span, f, h, v, w, prev, *held),
        [table(wall), table(span), block,
         pl.BlockSpec((step, ny, nz), lambda i: (i, 0, 0)), block, block, block]
        + [keep] * len(held),
        after,
        grid=(planes // step,),
        out_specs=[block, block, MARK_BLOCK],
        out_shape=[out, out, MARK],
        input_output_aliases={7 + k: k for k in range(len(held))},
        compiler_params=params(),
        cost_estimate=cost(6 * planes * ny * nz * (2 * ny + 2 * nz), planes * ny * nz * 22),
    )


def merge_kernel(rate, s_ref, next_ref, tend_ref, next_out, tend_out, mark_ref):
    mark_ref[...] = jnp.zeros_like(mark_ref)
    nx, step, nz = next_ref.shape
    coded = jnp.swapaxes(s_ref[...].astype(F32).reshape(step, nx, nz), 0, 1)
    add = DT_STEP * decode_stream(coded, rate)
    tend_out[...] = tend_ref[...] + add
    next_out[...] = next_ref[...] + GAMMA_RK * add


def merge(s, held, first_row, rate, after):
    nx, ny, nz = held[0].shape
    shares, each = s.shape[:2]
    per = STEP // each
    base = first_row // STEP
    block = pl.BlockSpec((nx, STEP, nz), lambda i: (0, base + i, 0))
    out = jax.ShapeDtypeStruct(held[0].shape, F32)
    return launch(
        functools.partial(merge_kernel, rate),
        (s, *held),
        [pl.BlockSpec((per, each, nx, nz), lambda i: (i, 0, 0, 0)), block, block],
        after,
        grid=(shares * each // STEP,),
        out_specs=[block, block, MARK_BLOCK],
        out_shape=[out, out, MARK],
        input_output_aliases={1: 0, 2: 1},
        compiler_params=params(),
        cost_estimate=cost(0, shares * each * nx * nz * 18),
    )


CHUNKS = (32,) * 6
PIECES = 4
ORDER = (
    "P0", "Y0", "P1", "Y1", "Y2", "Y3", "P2", "L0", "X0", "P3", "L1", "X1", "P4", "L2", "X2",
    "P5", "L3", "X3", "M0", "X4", "M1", "M2", "X5", "M3", "M4", "M5",
)


def body(px, pz, f, prev, u, v, w):
    nx, ny, nz = f.shape
    nxg = nx * px
    first, second = fourier_kernels(nxg, LENGTH_X)
    rate_bound = VELOCITY_BOUND * SCALAR_BOUND * np.abs(first).sum() + SCALAR_BOUND * np.abs(second).sum()
    rate = float(2 * CODE_TOP / np.log2(1.0 + 1.02 * rate_bound / STREAM_UNIT))
    k_first, k_second = circulant(first), circulant(second)
    z_first, z_second = (circulant(c) for c in fourier_kernels(nz, LENGTH_Z))
    span = jnp.asarray(two_terms(np.concatenate([z_first.T, z_second.T], axis=1)))
    walls = wall_table(ny * pz)
    mine = lax.axis_index("pz")
    wall_all = []
    for y in range(pz):
        rows = walls[y * ny:(y + 1) * ny]
        own = rows[:, y * ny:(y + 1) * ny]
        other = rows[:, (1 - y) * ny:(2 - y) * ny]
        wall_all.append(two_terms(np.concatenate([own, other], axis=1)))
    wall = lax.dynamic_index_in_dim(jnp.asarray(np.stack(wall_all)), mine, 0, keepdims=False)

    ring = px // 4
    quarter = nx * ring
    variants = []
    for order in ((1, 0, 2, 3), (2, 3, 1, 0)):
        pick = lambda m: np.concatenate(
            [np.concatenate([m[o * quarter:(o + 1) * quarter, q * quarter:(q + 1) * quarter] for q in order], axis=1)
             for o in order[:2]], axis=0)
        variants.append(np.stack([two_terms(pick(k_first)), two_terms(pick(k_second))], axis=1))
    level = lax.axis_index("px") // ring
    table = lax.dynamic_index_in_dim(jnp.asarray(np.stack(variants)), level // 2, 0, keepdims=False)
    outer = (level == 0) | (level == 3)
    groups = [[l * ring + r for r in range(ring)] for l in range(4)]
    hop = lambda pairs: [(a * ring + r, b * ring + r) for a, b in pairs for r in range(ring)]
    inward, across, outward = hop([(0, 1), (3, 2)]), hop([(1, 2), (2, 1)]), hop([(1, 0), (2, 3)])
    planes = nx // PIECES
    starts = [int(x) for x in np.concatenate([[0], np.cumsum(CHUNKS)])]

    made = {}
    last = ()

    def exchange(x):
        return lax.all_to_all(x, "px", 0, 0, axis_index_groups=groups, tiled=True)

    def after(names):
        return tuple(last) + tuple(made[n] for n in names.split())

    def send(name, x, pairs, axis="px"):
        with jax.named_scope("send_" + name):
            made[name] = lax.ppermute(x, axis, pairs)
        return made[name]

    def share(name, x):
        with jax.named_scope("share_" + name):
            made[name] = lax.all_to_all(x, "px", 0, 0, axis_index_groups=groups, tiled=True)
        return made[name]

    held = ()
    for word in ORDER:
        name, _, waits = word.partition(":")
        kind, c = name[0], int(name[1:])
        with jax.named_scope("kernel_" + name):
            if kind == "P":
                g, ut = pack(f, u, starts[c], CHUNKS[c], ring, after(waits))
                last = (g,)
            elif kind == "Y":
                h = code(f, c * planes, planes, after(waits))
                last = (h,)
            elif kind == "L":
                *held, mark = local(wall, span, f, made[f"y{c}"], v, w, prev, c * planes, held, after(waits))
                last = (mark,)
            elif kind == "X":
                fields = [made[f"{k}{c}"] for k in "gnab"]
                speeds = [made[f"{k}{c}"] for k in "uv"]
                s_own, s_near = stream(table, fields, speeds, rate, after(waits))
                last = (s_own,)
            else:
                *held, mark = merge(made[f"r{c}"], held, starts[c], rate, after(waits))
                last = (mark,)
        if kind == "P":
            g = share(f"g{c}", g)
            ut = share(f"u{c}", ut)
            near = send(f"n{c}", g, inward)
            send(f"a{c}", g, across)
            send(f"v{c}", ut, inward)
            send(f"b{c}", near, across)
        elif kind == "Y":
            send(f"y{c}", h, [(0, 1), (1, 0)], "pz")
        elif kind == "X":
            got = send(f"o{c}", s_near, outward)
            made[f"s{c}"] = s = jnp.where(outer, got, s_own)
            share(f"r{c}", s)
    return tuple(held)


def plain_wall(points):
    return jnp.asarray(wall_table(points), F32)


def plain_body(scalar_field, prev_tendency, velocity_u, velocity_v, velocity_w):
    highest = lax.Precision.HIGHEST
    z_tables = [circulant(c) for c in fourier_kernels(scalar_field.shape[2], LENGTH_Z)]
    z_first, z_diffusion = (
        jnp.einsum("ij,abj->abi", jnp.asarray(t, F32), scalar_field, precision=highest) for t in z_tables
    )
    normal = lax.all_to_all(scalar_field, "pz", split_axis=2, concat_axis=1, tiled=True)
    slope = jnp.einsum("ij,ajb->aib", plain_wall(normal.shape[1]), normal, precision=highest)
    slope = lax.all_to_all(slope, "pz", split_axis=1, concat_axis=2, tiled=True)
    pencil = lax.all_to_all(scalar_field, "px", split_axis=2, concat_axis=0, tiled=True)
    x_tables = [circulant(c) for c in fourier_kernels(pencil.shape[0], LENGTH_X)]
    x_first, x_diffusion = (
        lax.all_to_all(
            jnp.einsum("ij,jab->iab", jnp.asarray(t, F32), pencil, precision=highest),
            "px", split_axis=0, concat_axis=2, tiled=True,
        )
        for t in x_tables
    )
    forcing = (
        velocity_u.astype(F32) * x_first
        + x_diffusion
        + velocity_v.astype(F32) * slope
        + velocity_w.astype(F32) * z_first
        + z_diffusion
    )
    tendency = DT_STEP * forcing
    return scalar_field + GAMMA_RK * tendency + ZETA_RK * prev_tendency, tendency


def fits(px, pz, shape):
    nx, ny, nz = shape
    return px == 16 and pz == 2 and nx % 16 == 0 and ny == sum(CHUNKS) and nz % 128 == 0


def whole_body(px, pz, *arrays):
    if fits(px, pz, arrays[0].shape):
        return body(px, pz, *arrays)
    return plain_body(*arrays)


def solution(mesh):
    px, pz = mesh.shape["px"], mesh.shape["pz"]
    spec = P("px", "pz", None)
    return jax.shard_map(
        functools.partial(whole_body, px, pz),
        mesh=mesh,
        in_specs=(spec,) * 5,
        out_specs=(spec, spec),
        check_vma=False,
    )
```

```python
import functools

import jax
import jax.numpy as jnp
import ml_dtypes
import numpy as np
from jax import lax
from jax.experimental import pallas as pl
from jax.experimental.pallas import tpu as pltpu
from jax.sharding import PartitionSpec as P

KAPPA = 1.0 / (550.0 * 0.71)
DT_STEP = 0.005
GAMMA_RK = 8.0 / 15.0
ZETA_RK = -17.0 / 60.0
LENGTH_X = 4.0 * 3.141592653589793
LENGTH_Z = 4.0 * 3.141592653589793 / 3.0

F32 = jnp.float32
BF16 = jnp.bfloat16
VMEM = 56 << 20

SCALAR_BOUND = 6.0
VELOCITY_BOUND = 6.0
CODE_TOP = 120.0
SCALAR_RATE = CODE_TOP / (0.5 * SCALAR_BOUND)
STREAM_UNIT = 8.0
LOG2E = 1.4426950408889634


def wall_table(points):
    j = np.arange(points)
    angle = np.pi * j / (points - 1)
    node = np.cos(angle)
    weight = np.where((j == 0) | (j == points - 1), 2.0, 1.0)
    half = 0.5 * np.pi / (points - 1)
    gap = -2.0 * np.sin((j[:, None] + j[None, :]) * half) * np.sin((j[:, None] - j[None, :]) * half)
    gap[j, j] = 1.0
    parity = 1.0 - 2.0 * ((j[:, None] + j[None, :]) % 2)
    table = (np.sin(angle) ** 2)[:, None] * (weight[:, None] / weight[None, :]) * parity / gap
    table[j, j] = -0.5 * node
    table[0, :] = 0.0
    table[-1, :] = 0.0
    return table


def fourier_kernels(extent, length):
    mode = np.arange(extent // 3)
    wave = mode * (2.0 * np.pi / length)
    phase = 2.0 * np.pi * (np.outer(np.arange(extent), mode) % extent) / extent
    first = -(2.0 / extent) * (np.sin(phase) @ wave)
    second = -(2.0 * KAPPA / extent) * (np.cos(phase) @ (wave * wave))
    return first, second


def circulant(column):
    n = column.shape[0]
    i = np.arange(n)
    return column[(i[:, None] - i[None, :]) % n]


def two_terms(table):
    table = np.asarray(table, np.float32)
    high = table.astype(ml_dtypes.bfloat16)
    low = (table - high.astype(np.float32)).astype(ml_dtypes.bfloat16)
    return np.stack([high, low])


def encode_scalar(x):
    size = jnp.exp2(SCALAR_RATE * jnp.abs(x) - CODE_TOP)
    return jnp.where(x < 0, -size, size)


def decode_scalar(b):
    size = (jnp.log(jnp.abs(b)) * LOG2E + CODE_TOP) * (1.0 / SCALAR_RATE)
    return jnp.where(b < 0, -size, size)


def encode_stream(x, rate):
    size = jnp.exp2((rate * LOG2E) * jnp.log(1.0 + jnp.abs(x) * (1.0 / STREAM_UNIT)) - CODE_TOP)
    return jnp.where(x < 0, -size, size)


def decode_stream(b, rate):
    size = STREAM_UNIT * (jnp.exp2((jnp.log(jnp.abs(b)) * LOG2E + CODE_TOP) * (1.0 / rate)) - 1.0)
    return jnp.where(b < 0, -size, size)


def split(x):
    high = x.astype(BF16)
    return high, (x - high.astype(F32)).astype(BF16)


def dot(a, b):
    return jnp.dot(a, b, preferred_element_type=F32)


def dot3(a_high, a_low, b_high, b_low):
    return dot(a_high, b_high) + dot(a_high, b_low) + dot(a_low, b_high)


def params(**kw):
    return pltpu.CompilerParams(vmem_limit_bytes=VMEM, **kw)


COST = 1.0


def cost(flops, moved):
    return pl.CostEstimate(flops=int(COST * flops), bytes_accessed=int(COST * moved), transcendentals=0)


def launch(kernel, operands, in_specs, after, **kw):
    count, extra = len(operands), len(after)

    def run(*refs):
        kernel(*refs[:count], *refs[count + extra:])

    return pl.pallas_call(
        run,
        in_specs=list(in_specs) + [pl.BlockSpec(memory_space=pl.ANY)] * extra,
        **kw,
    )(*operands, *after)


STEP = 16
MARK = jax.ShapeDtypeStruct((8, 128), F32)
MARK_BLOCK = pl.BlockSpec((8, 128), lambda i: (0, 0))


def pack_kernel(f_ref, u_ref, g_ref, w_ref):
    code = encode_scalar(f_ref[...])
    g_ref[...] = jnp.swapaxes(code, 0, 1).astype(BF16).reshape(g_ref.shape)
    u = jnp.swapaxes(u_ref[...].astype(F32), 0, 1)
    w_ref[...] = u.astype(BF16).reshape(w_ref.shape)


def pack(f, u, first_row, rows, shares, after):
    nx, ny, nz = f.shape
    each = rows // shares
    per = STEP // each
    out = jax.ShapeDtypeStruct((shares, each, nx, nz), BF16)
    base = first_row // STEP
    return launch(
        pack_kernel,
        (f, u),
        [pl.BlockSpec((nx, STEP, nz), lambda i: (0, base + i, 0))] * 2,
        after,
        grid=(rows // STEP,),
        out_specs=[pl.BlockSpec((per, each, nx, nz), lambda i: (i, 0, 0, 0))] * 2,
        out_shape=[out, out],
        compiler_params=params(),
        cost_estimate=cost(0, rows * nx * nz * 10),
    )


def code_kernel(f_ref, h_ref):
    h_ref[...] = encode_scalar(f_ref[...]).astype(BF16)


def code(f, first, planes, after):
    _, ny, nz = f.shape
    step = 4
    base = first // step
    return launch(
        code_kernel,
        (f,),
        [pl.BlockSpec((step, ny, nz), lambda i: (base + i, 0, 0))],
        after,
        grid=(planes // step,),
        out_specs=pl.BlockSpec((step, ny, nz), lambda i: (i, 0, 0)),
        out_shape=jax.ShapeDtypeStruct((planes, ny, nz), BF16),
        compiler_params=params(),
        cost_estimate=cost(0, planes * ny * nz * 6),
    )


def stream_kernel(n_in, n_out, rate, table_ref, *refs):
    f_refs, u_refs, s_refs = refs[:n_in], refs[n_in:n_in + n_out], refs[n_in + n_out:]
    rows = refs[0].shape[1]
    nz = refs[0].shape[3]
    columns = []
    for k in range(rows):
        blocks = [r[:, k].astype(F32).reshape(-1, nz) for r in f_refs]
        columns.append(jnp.concatenate(blocks, axis=0) if n_in > 1 else blocks[0])
    field = decode_scalar(jnp.concatenate(columns, axis=1))
    high, low = split(field)
    deep = table_ref.shape[3]
    both = dot(table_ref[...].reshape(-1, deep), high)
    tall = both.shape[0] // 2
    spread = both[:tall] + both[tall:] + dot(table_ref[0].reshape(tall, deep), low)
    half = tall // (2 * n_out)
    for o in range(n_out):
        first, second = spread[o * half:(o + 1) * half], spread[tall // 2 + o * half:tall // 2 + (o + 1) * half]
        for k in range(rows):
            cols = slice(k * nz, (k + 1) * nz)
            u = u_refs[o][:, k].astype(F32).reshape(half, nz)
            value = u * first[:, cols] + second[:, cols]
            s_refs[o][:, k] = encode_stream(value, rate).astype(BF16).reshape(s_refs[o].shape[0], -1, nz)


def stream(table, fields, speeds, rate, after):
    parts, rows, nx, nz = fields[0].shape
    n_in, n_out = len(fields), len(speeds)
    step = 2 if rows % 2 == 0 else 1
    block = pl.BlockSpec((parts, step, nx, nz), lambda i: (0, i, 0, 0))
    whole = pl.BlockSpec(table.shape, lambda i: (0, 0, 0, 0), pipeline_mode=pl.Buffered(1))
    points = table.shape[2] * table.shape[3]
    moved = 2 * (n_in + 2 * n_out) * parts * rows * nx * nz
    return launch(
        functools.partial(stream_kernel, n_in, n_out, rate),
        (table, *fields, *speeds),
        [whole] + [block] * (n_in + n_out),
        after,
        grid=(rows // step,),
        out_specs=[block] * n_out,
        out_shape=[jax.ShapeDtypeStruct(fields[0].shape, BF16)] * n_out,
        compiler_params=params(),
        cost_estimate=cost(12 * points * rows * nz, moved),
    )


def local_kernel(wall_ref, span_ref, f_ref, h_ref, v_ref, w_ref, p_ref, *refs):
    next_ref, tend_ref, mark_ref = refs[-3:]
    mark_ref[...] = jnp.zeros_like(mark_ref)
    planes, ny, nz = f_ref.shape
    own = f_ref[...]
    other = decode_scalar(h_ref[...].astype(F32))
    own_high, own_low = split(own)
    other_high, other_low = split(other)

    def stack(a, b):
        return jnp.concatenate(
            [jnp.concatenate([a[x], b[x]], axis=0) for x in range(planes)], axis=1
        )

    y_high, y_low = stack(own_high, other_high), stack(own_low, other_low)
    both = dot(wall_ref[...].reshape(2 * ny, -1), y_high)
    slope = both[:ny] + both[ny:] + dot(wall_ref[0], y_low)
    z_high, z_low = own_high.reshape(-1, nz), own_low.reshape(-1, nz)
    span = dot3(z_high, z_low, span_ref[0], span_ref[1])
    for x in range(planes):
        rows = slice(x * ny, (x + 1) * ny)
        forcing = (
            v_ref[x].astype(F32) * slope[:, x * nz:(x + 1) * nz]
            + w_ref[x].astype(F32) * span[rows, :nz]
            + span[rows, nz:]
        )
        tendency = DT_STEP * forcing
        tend_ref[x] = tendency
        next_ref[x] = own[x] + GAMMA_RK * tendency + ZETA_RK * p_ref[x]


def local(wall, span, f, h, v, w, prev, first, held, after):
    nx, ny, nz = f.shape
    planes = h.shape[0]
    step = 2
    base = first // step
    block = pl.BlockSpec((step, ny, nz), lambda i: (base + i, 0, 0))
    table = lambda t: pl.BlockSpec(t.shape, lambda i: (0, 0, 0), pipeline_mode=pl.Buffered(1))
    out = jax.ShapeDtypeStruct(f.shape, F32)
    keep = pl.BlockSpec(memory_space=pl.ANY)
    return launch(
        local_kernel,
        (wall, span, f, h, v, w, prev, *held),
        [table(wall), table(span), block,
         pl.BlockSpec((step, ny, nz), lambda i: (i, 0, 0)), block, block, block]
        + [keep] * len(held),
        after,
        grid=(planes // step,),
        out_specs=[block, block, MARK_BLOCK],
        out_shape=[out, out, MARK],
        input_output_aliases={7 + k: k for k in range(len(held))},
        compiler_params=params(),
        cost_estimate=cost(6 * planes * ny * nz * (2 * ny + 2 * nz), planes * ny * nz * 22),
    )


def merge_kernel(rate, s_ref, next_ref, tend_ref, next_out, tend_out, mark_ref):
    mark_ref[...] = jnp.zeros_like(mark_ref)
    nx, step, nz = next_ref.shape
    coded = jnp.swapaxes(s_ref[...].astype(F32).reshape(step, nx, nz), 0, 1)
    add = DT_STEP * decode_stream(coded, rate)
    tend_out[...] = tend_ref[...] + add
    next_out[...] = next_ref[...] + GAMMA_RK * add


def merge(s, held, first_row, rate, after):
    nx, ny, nz = held[0].shape
    shares, each = s.shape[:2]
    per = STEP // each
    base = first_row // STEP
    block = pl.BlockSpec((nx, STEP, nz), lambda i: (0, base + i, 0))
    out = jax.ShapeDtypeStruct(held[0].shape, F32)
    return launch(
        functools.partial(merge_kernel, rate),
        (s, *held),
        [pl.BlockSpec((per, each, nx, nz), lambda i: (i, 0, 0, 0)), block, block],
        after,
        grid=(shares * each // STEP,),
        out_specs=[block, block, MARK_BLOCK],
        out_shape=[out, out, MARK],
        input_output_aliases={1: 0, 2: 1},
        compiler_params=params(),
        cost_estimate=cost(0, shares * each * nx * nz * 18),
    )


CHUNKS = (32,) * 6
PIECES = 4
ORDER = (
    "P0", "Y0", "P1", "Y1", "Y2", "Y3", "P2", "L0", "X0", "P3", "L1", "X1", "P4", "L2", "X2",
    "P5", "L3", "X3", "M0", "X4", "M1", "M2", "X5", "M3", "M4", "M5",
)


def body(px, pz, f, prev, u, v, w):
    nx, ny, nz = f.shape
    nxg = nx * px
    first, second = fourier_kernels(nxg, LENGTH_X)
    rate_bound = VELOCITY_BOUND * SCALAR_BOUND * np.abs(first).sum() + SCALAR_BOUND * np.abs(second).sum()
    rate = float(2 * CODE_TOP / np.log2(1.0 + 1.02 * rate_bound / STREAM_UNIT))
    k_first, k_second = circulant(first), circulant(second)
    z_first, z_second = (circulant(c) for c in fourier_kernels(nz, LENGTH_Z))
    span = jnp.asarray(two_terms(np.concatenate([z_first.T, z_second.T], axis=1)))
    walls = wall_table(ny * pz)
    mine = lax.axis_index("pz")
    wall_all = []
    for y in range(pz):
        rows = walls[y * ny:(y + 1) * ny]
        own = rows[:, y * ny:(y + 1) * ny]
        other = rows[:, (1 - y) * ny:(2 - y) * ny]
        wall_all.append(two_terms(np.concatenate([own, other], axis=1)))
    wall = lax.dynamic_index_in_dim(jnp.asarray(np.stack(wall_all)), mine, 0, keepdims=False)

    ring = px // 4
    quarter = nx * ring
    variants = []
    for order in ((1, 0, 2, 3), (2, 3, 1, 0)):
        pick = lambda m: np.concatenate(
            [np.concatenate([m[o * quarter:(o + 1) * quarter, q * quarter:(q + 1) * quarter] for q in order], axis=1)
             for o in order[:2]], axis=0)
        variants.append(np.stack([two_terms(pick(k_first)), two_terms(pick(k_second))], axis=1))
    level = lax.axis_index("px") // ring
    table = lax.dynamic_index_in_dim(jnp.asarray(np.stack(variants)), level // 2, 0, keepdims=False)
    outer = (level == 0) | (level == 3)
    groups = [[l * ring + r for r in range(ring)] for l in range(4)]
    hop = lambda pairs: [(a * ring + r, b * ring + r) for a, b in pairs for r in range(ring)]
    inward, across, outward = hop([(0, 1), (3, 2)]), hop([(1, 2), (2, 1)]), hop([(1, 0), (2, 3)])
    planes = nx // PIECES
    starts = [int(x) for x in np.concatenate([[0], np.cumsum(CHUNKS)])]

    made = {}
    last = ()

    def exchange(x):
        return lax.all_to_all(x, "px", 0, 0, axis_index_groups=groups, tiled=True)

    def after(names):
        return tuple(last) + tuple(made[n] for n in names.split())

    def send(name, x, pairs, axis="px"):
        with jax.named_scope("send_" + name):
            made[name] = lax.ppermute(x, axis, pairs)
        return made[name]

    def share(name, x):
        with jax.named_scope("share_" + name):
            made[name] = lax.all_to_all(x, "px", 0, 0, axis_index_groups=groups, tiled=True)
        return made[name]

    held = ()
    for word in ORDER:
        name, _, waits = word.partition(":")
        kind, c = name[0], int(name[1:])
        with jax.named_scope("kernel_" + name):
            if kind == "P":
                g, ut = pack(f, u, starts[c], CHUNKS[c], ring, after(waits))
                last = (g,)
            elif kind == "Y":
                h = code(f, c * planes, planes, after(waits))
                last = (h,)
            elif kind == "L":
                *held, mark = local(wall, span, f, made[f"y{c}"], v, w, prev, c * planes, held, after(waits))
                last = (mark,)
            elif kind == "X":
                fields = [made[f"{k}{c}"] for k in "gnab"]
                speeds = [made[f"{k}{c}"] for k in "uv"]
                s_own, s_near = stream(table, fields, speeds, rate, after(waits))
                last = (s_own,)
            else:
                *held, mark = merge(made[f"r{c}"], held, starts[c], rate, after(waits))
                last = (mark,)
        if kind == "P":
            g = share(f"g{c}", g)
            ut = share(f"u{c}", ut)
            near = send(f"n{c}", g, inward)
            send(f"a{c}", g, across)
            send(f"v{c}", ut, inward)
            send(f"b{c}", near, across)
        elif kind == "Y":
            send(f"y{c}", h, [(0, 1), (1, 0)], "pz")
        elif kind == "X":
            got = send(f"o{c}", s_near, outward)
            made[f"s{c}"] = s = jnp.where(outer, got, s_own)
            share(f"r{c}", s)
    return tuple(held)


def plain_wall(points):
    return jnp.asarray(wall_table(points), F32)


def plain_body(scalar_field, prev_tendency, velocity_u, velocity_v, velocity_w):
    highest = lax.Precision.HIGHEST
    z_tables = [circulant(c) for c in fourier_kernels(scalar_field.shape[2], LENGTH_Z)]
    z_first, z_diffusion = (
        jnp.einsum("ij,abj->abi", jnp.asarray(t, F32), scalar_field, precision=highest) for t in z_tables
    )
    normal = lax.all_to_all(scalar_field, "pz", split_axis=2, concat_axis=1, tiled=True)
    slope = jnp.einsum("ij,ajb->aib", plain_wall(normal.shape[1]), normal, precision=highest)
    slope = lax.all_to_all(slope, "pz", split_axis=1, concat_axis=2, tiled=True)
    pencil = lax.all_to_all(scalar_field, "px", split_axis=2, concat_axis=0, tiled=True)
    x_tables = [circulant(c) for c in fourier_kernels(pencil.shape[0], LENGTH_X)]
    x_first, x_diffusion = (
        lax.all_to_all(
            jnp.einsum("ij,jab->iab", jnp.asarray(t, F32), pencil, precision=highest),
            "px", split_axis=0, concat_axis=2, tiled=True,
        )
        for t in x_tables
    )
    forcing = (
        velocity_u.astype(F32) * x_first
        + x_diffusion
        + velocity_v.astype(F32) * slope
        + velocity_w.astype(F32) * z_first
        + z_diffusion
    )
    tendency = DT_STEP * forcing
    return scalar_field + GAMMA_RK * tendency + ZETA_RK * prev_tendency, tendency


def fits(px, pz, shape):
    nx, ny, nz = shape
    return px == 16 and pz == 2 and nx % 16 == 0 and ny == sum(CHUNKS) and nz % 128 == 0


def whole_body(px, pz, *arrays):
    if fits(px, pz, arrays[0].shape):
        return body(px, pz, *arrays)
    return plain_body(*arrays)


def solution(mesh):
    px, pz = mesh.shape["px"], mesh.shape["pz"]
    spec = P("px", "pz", None)
    return jax.shard_map(
        functools.partial(whole_body, px, pz),
        mesh=mesh,
        in_specs=(spec,) * 5,
        out_specs=(spec, spec),
        check_vma=False,
    )
```

```python
import functools

import jax
import jax.numpy as jnp
import ml_dtypes
import numpy as np
from jax import lax
from jax.experimental import pallas as pl
from jax.experimental.pallas import tpu as pltpu
from jax.sharding import PartitionSpec as P

KAPPA = 1.0 / (550.0 * 0.71)
DT_STEP = 0.005
GAMMA_RK = 8.0 / 15.0
ZETA_RK = -17.0 / 60.0
LENGTH_X = 4.0 * 3.141592653589793
LENGTH_Z = 4.0 * 3.141592653589793 / 3.0

F32 = jnp.float32
BF16 = jnp.bfloat16
VMEM = 56 << 20

SCALAR_BOUND = 6.0
VELOCITY_BOUND = 6.0
CODE_TOP = 120.0
SCALAR_RATE = CODE_TOP / (0.5 * SCALAR_BOUND)
STREAM_UNIT = 8.0
LOG2E = 1.4426950408889634


def wall_table(points):
    j = np.arange(points)
    angle = np.pi * j / (points - 1)
    node = np.cos(angle)
    weight = np.where((j == 0) | (j == points - 1), 2.0, 1.0)
    half = 0.5 * np.pi / (points - 1)
    gap = -2.0 * np.sin((j[:, None] + j[None, :]) * half) * np.sin((j[:, None] - j[None, :]) * half)
    gap[j, j] = 1.0
    parity = 1.0 - 2.0 * ((j[:, None] + j[None, :]) % 2)
    table = (np.sin(angle) ** 2)[:, None] * (weight[:, None] / weight[None, :]) * parity / gap
    table[j, j] = -0.5 * node
    table[0, :] = 0.0
    table[-1, :] = 0.0
    return table


def fourier_kernels(extent, length):
    mode = np.arange(extent // 3)
    wave = mode * (2.0 * np.pi / length)
    phase = 2.0 * np.pi * (np.outer(np.arange(extent), mode) % extent) / extent
    first = -(2.0 / extent) * (np.sin(phase) @ wave)
    second = -(2.0 * KAPPA / extent) * (np.cos(phase) @ (wave * wave))
    return first, second


def circulant(column):
    n = column.shape[0]
    i = np.arange(n)
    return column[(i[:, None] - i[None, :]) % n]


def two_terms(table):
    table = np.asarray(table, np.float32)
    high = table.astype(ml_dtypes.bfloat16)
    low = (table - high.astype(np.float32)).astype(ml_dtypes.bfloat16)
    return np.stack([high, low])


def encode_scalar(x):
    size = jnp.exp2(SCALAR_RATE * jnp.abs(x) - CODE_TOP)
    return jnp.where(x < 0, -size, size)


def decode_scalar(b):
    size = (jnp.log(jnp.abs(b)) * LOG2E + CODE_TOP) * (1.0 / SCALAR_RATE)
    return jnp.where(b < 0, -size, size)


def encode_stream(x, rate):
    size = jnp.exp2((rate * LOG2E) * jnp.log(1.0 + jnp.abs(x) * (1.0 / STREAM_UNIT)) - CODE_TOP)
    return jnp.where(x < 0, -size, size)


def decode_stream(b, rate):
    size = STREAM_UNIT * (jnp.exp2((jnp.log(jnp.abs(b)) * LOG2E + CODE_TOP) * (1.0 / rate)) - 1.0)
    return jnp.where(b < 0, -size, size)


def split(x):
    high = x.astype(BF16)
    return high, (x - high.astype(F32)).astype(BF16)


def dot(a, b):
    return jnp.dot(a, b, preferred_element_type=F32)


def dot3(a_high, a_low, b_high, b_low):
    return dot(a_high, b_high) + dot(a_high, b_low) + dot(a_low, b_high)


def params(**kw):
    return pltpu.CompilerParams(vmem_limit_bytes=VMEM, **kw)


COST = 1.0


def cost(flops, moved):
    return pl.CostEstimate(flops=int(COST * flops), bytes_accessed=int(COST * moved), transcendentals=0)


def launch(kernel, operands, in_specs, after, **kw):
    count, extra = len(operands), len(after)

    def run(*refs):
        kernel(*refs[:count], *refs[count + extra:])

    return pl.pallas_call(
        run,
        in_specs=list(in_specs) + [pl.BlockSpec(memory_space=pl.ANY)] * extra,
        **kw,
    )(*operands, *after)


STEP = 16
MARK = jax.ShapeDtypeStruct((8, 128), F32)
MARK_BLOCK = pl.BlockSpec((8, 128), lambda i: (0, 0))


def pack_kernel(f_ref, u_ref, g_ref, w_ref):
    code = encode_scalar(f_ref[...])
    g_ref[...] = jnp.swapaxes(code, 0, 1).astype(BF16).reshape(g_ref.shape)
    u = jnp.swapaxes(u_ref[...].astype(F32), 0, 1)
    w_ref[...] = u.astype(BF16).reshape(w_ref.shape)


def pack(f, u, first_row, rows, shares, after):
    nx, ny, nz = f.shape
    each = rows // shares
    per = STEP // each
    out = jax.ShapeDtypeStruct((shares, each, nx, nz), BF16)
    base = first_row // STEP
    return launch(
        pack_kernel,
        (f, u),
        [pl.BlockSpec((nx, STEP, nz), lambda i: (0, base + i, 0))] * 2,
        after,
        grid=(rows // STEP,),
        out_specs=[pl.BlockSpec((per, each, nx, nz), lambda i: (i, 0, 0, 0))] * 2,
        out_shape=[out, out],
        compiler_params=params(),
        cost_estimate=cost(0, rows * nx * nz * 10),
    )


def code_kernel(f_ref, h_ref):
    h_ref[...] = encode_scalar(f_ref[...]).astype(BF16)


def code(f, first, planes, after):
    _, ny, nz = f.shape
    step = 4
    base = first // step
    return launch(
        code_kernel,
        (f,),
        [pl.BlockSpec((step, ny, nz), lambda i: (base + i, 0, 0))],
        after,
        grid=(planes // step,),
        out_specs=pl.BlockSpec((step, ny, nz), lambda i: (i, 0, 0)),
        out_shape=jax.ShapeDtypeStruct((planes, ny, nz), BF16),
        compiler_params=params(),
        cost_estimate=cost(0, planes * ny * nz * 6),
    )


def stream_kernel(n_in, n_out, rate, table_ref, *refs):
    f_refs, u_refs, s_refs = refs[:n_in], refs[n_in:n_in + n_out], refs[n_in + n_out:]
    rows = refs[0].shape[1]
    nz = refs[0].shape[3]
    columns = []
    for k in range(rows):
        blocks = [r[:, k].astype(F32).reshape(-1, nz) for r in f_refs]
        columns.append(jnp.concatenate(blocks, axis=0) if n_in > 1 else blocks[0])
    field = decode_scalar(jnp.concatenate(columns, axis=1))
    high, low = split(field)
    deep = table_ref.shape[3]
    both = dot(table_ref[...].reshape(-1, deep), high)
    tall = both.shape[0] // 2
    spread = both[:tall] + both[tall:] + dot(table_ref[0].reshape(tall, deep), low)
    half = tall // (2 * n_out)
    for o in range(n_out):
        first, second = spread[o * half:(o + 1) * half], spread[tall // 2 + o * half:tall // 2 + (o + 1) * half]
        for k in range(rows):
            cols = slice(k * nz, (k + 1) * nz)
            u = u_refs[o][:, k].astype(F32).reshape(half, nz)
            value = u * first[:, cols] + second[:, cols]
            s_refs[o][:, k] = encode_stream(value, rate).astype(BF16).reshape(s_refs[o].shape[0], -1, nz)


def stream(table, fields, speeds, rate, after):
    parts, rows, nx, nz = fields[0].shape
    n_in, n_out = len(fields), len(speeds)
    step = 2 if rows % 2 == 0 else 1
    block = pl.BlockSpec((parts, step, nx, nz), lambda i: (0, i, 0, 0))
    whole = pl.BlockSpec(table.shape, lambda i: (0, 0, 0, 0), pipeline_mode=pl.Buffered(1))
    points = table.shape[2] * table.shape[3]
    moved = 2 * (n_in + 2 * n_out) * parts * rows * nx * nz
    return launch(
        functools.partial(stream_kernel, n_in, n_out, rate),
        (table, *fields, *speeds),
        [whole] + [block] * (n_in + n_out),
        after,
        grid=(rows // step,),
        out_specs=[block] * n_out,
        out_shape=[jax.ShapeDtypeStruct(fields[0].shape, BF16)] * n_out,
        compiler_params=params(),
        cost_estimate=cost(12 * points * rows * nz, moved),
    )


def local_kernel(wall_ref, span_ref, f_ref, h_ref, v_ref, w_ref, p_ref, *refs):
    next_ref, tend_ref, mark_ref = refs[-3:]
    mark_ref[...] = jnp.zeros_like(mark_ref)
    planes, ny, nz = f_ref.shape
    own = f_ref[...]
    other = decode_scalar(h_ref[...].astype(F32))
    own_high, own_low = split(own)
    other_high, other_low = split(other)

    def stack(a, b):
        return jnp.concatenate(
            [jnp.concatenate([a[x], b[x]], axis=0) for x in range(planes)], axis=1
        )

    y_high, y_low = stack(own_high, other_high), stack(own_low, other_low)
    both = dot(wall_ref[...].reshape(2 * ny, -1), y_high)
    slope = both[:ny] + both[ny:] + dot(wall_ref[0], y_low)
    z_high, z_low = own_high.reshape(-1, nz), own_low.reshape(-1, nz)
    span = dot3(z_high, z_low, span_ref[0], span_ref[1])
    for x in range(planes):
        rows = slice(x * ny, (x + 1) * ny)
        forcing = (
            v_ref[x].astype(F32) * slope[:, x * nz:(x + 1) * nz]
            + w_ref[x].astype(F32) * span[rows, :nz]
            + span[rows, nz:]
        )
        tendency = DT_STEP * forcing
        tend_ref[x] = tendency
        next_ref[x] = own[x] + GAMMA_RK * tendency + ZETA_RK * p_ref[x]


def local(wall, span, f, h, v, w, prev, first, held, after):
    nx, ny, nz = f.shape
    planes = h.shape[0]
    step = 2
    base = first // step
    block = pl.BlockSpec((step, ny, nz), lambda i: (base + i, 0, 0))
    table = lambda t: pl.BlockSpec(t.shape, lambda i: (0, 0, 0), pipeline_mode=pl.Buffered(1))
    out = jax.ShapeDtypeStruct(f.shape, F32)
    keep = pl.BlockSpec(memory_space=pl.ANY)
    return launch(
        local_kernel,
        (wall, span, f, h, v, w, prev, *held),
        [table(wall), table(span), block,
         pl.BlockSpec((step, ny, nz), lambda i: (i, 0, 0)), block, block, block]
        + [keep] * len(held),
        after,
        grid=(planes // step,),
        out_specs=[block, block, MARK_BLOCK],
        out_shape=[out, out, MARK],
        input_output_aliases={7 + k: k for k in range(len(held))},
        compiler_params=params(),
        cost_estimate=cost(6 * planes * ny * nz * (2 * ny + 2 * nz), planes * ny * nz * 22),
    )


def merge_kernel(rate, s_ref, next_ref, tend_ref, next_out, tend_out, mark_ref):
    mark_ref[...] = jnp.zeros_like(mark_ref)
    nx, step, nz = next_ref.shape
    coded = jnp.swapaxes(s_ref[...].astype(F32).reshape(step, nx, nz), 0, 1)
    add = DT_STEP * decode_stream(coded, rate)
    tend_out[...] = tend_ref[...] + add
    next_out[...] = next_ref[...] + GAMMA_RK * add


def merge(s, held, first_row, rate, after):
    nx, ny, nz = held[0].shape
    shares, each = s.shape[:2]
    per = STEP // each
    base = first_row // STEP
    block = pl.BlockSpec((nx, STEP, nz), lambda i: (0, base + i, 0))
    out = jax.ShapeDtypeStruct(held[0].shape, F32)
    return launch(
        functools.partial(merge_kernel, rate),
        (s, *held),
        [pl.BlockSpec((per, each, nx, nz), lambda i: (i, 0, 0, 0)), block, block],
        after,
        grid=(shares * each // STEP,),
        out_specs=[block, block, MARK_BLOCK],
        out_shape=[out, out, MARK],
        input_output_aliases={1: 0, 2: 1},
        compiler_params=params(),
        cost_estimate=cost(0, shares * each * nx * nz * 18),
    )


CHUNKS = (32,) * 6
PIECES = 4
ORDER = (
    "P0", "Y0", "P1", "Y1", "Y2", "Y3", "P2", "L0", "X0", "P3", "L1", "X1", "P4", "L2", "X2",
    "P5:a3", "L3", "X3", "M0", "X4", "M1", "M2", "X5", "M3", "M4", "M5",
)


def body(px, pz, f, prev, u, v, w):
    nx, ny, nz = f.shape
    nxg = nx * px
    first, second = fourier_kernels(nxg, LENGTH_X)
    rate_bound = VELOCITY_BOUND * SCALAR_BOUND * np.abs(first).sum() + SCALAR_BOUND * np.abs(second).sum()
    rate = float(2 * CODE_TOP / np.log2(1.0 + 1.02 * rate_bound / STREAM_UNIT))
    k_first, k_second = circulant(first), circulant(second)
    z_first, z_second = (circulant(c) for c in fourier_kernels(nz, LENGTH_Z))
    span = jnp.asarray(two_terms(np.concatenate([z_first.T, z_second.T], axis=1)))
    walls = wall_table(ny * pz)
    mine = lax.axis_index("pz")
    wall_all = []
    for y in range(pz):
        rows = walls[y * ny:(y + 1) * ny]
        own = rows[:, y * ny:(y + 1) * ny]
        other = rows[:, (1 - y) * ny:(2 - y) * ny]
        wall_all.append(two_terms(np.concatenate([own, other], axis=1)))
    wall = lax.dynamic_index_in_dim(jnp.asarray(np.stack(wall_all)), mine, 0, keepdims=False)

    ring = px // 4
    quarter = nx * ring
    variants = []
    for order in ((1, 0, 2, 3), (2, 3, 1, 0)):
        pick = lambda m: np.concatenate(
            [np.concatenate([m[o * quarter:(o + 1) * quarter, q * quarter:(q + 1) * quarter] for q in order], axis=1)
             for o in order[:2]], axis=0)
        variants.append(np.stack([two_terms(pick(k_first)), two_terms(pick(k_second))], axis=1))
    level = lax.axis_index("px") // ring
    table = lax.dynamic_index_in_dim(jnp.asarray(np.stack(variants)), level // 2, 0, keepdims=False)
    outer = (level == 0) | (level == 3)
    groups = [[l * ring + r for r in range(ring)] for l in range(4)]
    hop = lambda pairs: [(a * ring + r, b * ring + r) for a, b in pairs for r in range(ring)]
    inward, across, outward = hop([(0, 1), (3, 2)]), hop([(1, 2), (2, 1)]), hop([(1, 0), (2, 3)])
    planes = nx // PIECES
    starts = [int(x) for x in np.concatenate([[0], np.cumsum(CHUNKS)])]

    made = {}
    last = ()

    def exchange(x):
        return lax.all_to_all(x, "px", 0, 0, axis_index_groups=groups, tiled=True)

    def after(names):
        return tuple(last) + tuple(made[n] for n in names.split())

    def send(name, x, pairs, axis="px"):
        with jax.named_scope("send_" + name):
            made[name] = lax.ppermute(x, axis, pairs)
        return made[name]

    def share(name, x):
        with jax.named_scope("share_" + name):
            made[name] = lax.all_to_all(x, "px", 0, 0, axis_index_groups=groups, tiled=True)
        return made[name]

    held = ()
    for word in ORDER:
        name, _, waits = word.partition(":")
        kind, c = name[0], int(name[1:])
        with jax.named_scope("kernel_" + name):
            if kind == "P":
                g, ut = pack(f, u, starts[c], CHUNKS[c], ring, after(waits))
                last = (g,)
            elif kind == "Y":
                h = code(f, c * planes, planes, after(waits))
                last = (h,)
            elif kind == "L":
                *held, mark = local(wall, span, f, made[f"y{c}"], v, w, prev, c * planes, held, after(waits))
                last = (mark,)
            elif kind == "X":
                fields = [made[f"{k}{c}"] for k in "gnab"]
                speeds = [made[f"{k}{c}"] for k in "uv"]
                s_own, s_near = stream(table, fields, speeds, rate, after(waits))
                last = (s_own,)
            else:
                *held, mark = merge(made[f"r{c}"], held, starts[c], rate, after(waits))
                last = (mark,)
        if kind == "P":
            g = share(f"g{c}", g)
            ut = share(f"u{c}", ut)
            near = send(f"n{c}", g, inward)
            send(f"a{c}", g, across)
            send(f"v{c}", ut, inward)
            send(f"b{c}", near, across)
        elif kind == "Y":
            send(f"y{c}", h, [(0, 1), (1, 0)], "pz")
        elif kind == "X":
            got = send(f"o{c}", s_near, outward)
            made[f"s{c}"] = s = jnp.where(outer, got, s_own)
            share(f"r{c}", s)
    return tuple(held)


def plain_wall(points):
    return jnp.asarray(wall_table(points), F32)


def plain_body(scalar_field, prev_tendency, velocity_u, velocity_v, velocity_w):
    highest = lax.Precision.HIGHEST
    z_tables = [circulant(c) for c in fourier_kernels(scalar_field.shape[2], LENGTH_Z)]
    z_first, z_diffusion = (
        jnp.einsum("ij,abj->abi", jnp.asarray(t, F32), scalar_field, precision=highest) for t in z_tables
    )
    normal = lax.all_to_all(scalar_field, "pz", split_axis=2, concat_axis=1, tiled=True)
    slope = jnp.einsum("ij,ajb->aib", plain_wall(normal.shape[1]), normal, precision=highest)
    slope = lax.all_to_all(slope, "pz", split_axis=1, concat_axis=2, tiled=True)
    pencil = lax.all_to_all(scalar_field, "px", split_axis=2, concat_axis=0, tiled=True)
    x_tables = [circulant(c) for c in fourier_kernels(pencil.shape[0], LENGTH_X)]
    x_first, x_diffusion = (
        lax.all_to_all(
            jnp.einsum("ij,jab->iab", jnp.asarray(t, F32), pencil, precision=highest),
            "px", split_axis=0, concat_axis=2, tiled=True,
        )
        for t in x_tables
    )
    forcing = (
        velocity_u.astype(F32) * x_first
        + x_diffusion
        + velocity_v.astype(F32) * slope
        + velocity_w.astype(F32) * z_first
        + z_diffusion
    )
    tendency = DT_STEP * forcing
    return scalar_field + GAMMA_RK * tendency + ZETA_RK * prev_tendency, tendency


def fits(px, pz, shape):
    nx, ny, nz = shape
    return px == 16 and pz == 2 and nx % 16 == 0 and ny == sum(CHUNKS) and nz % 128 == 0


def whole_body(px, pz, *arrays):
    if fits(px, pz, arrays[0].shape):
        return body(px, pz, *arrays)
    return plain_body(*arrays)


def solution(mesh):
    px, pz = mesh.shape["px"], mesh.shape["pz"]
    spec = P("px", "pz", None)
    return jax.shard_map(
        functools.partial(whole_body, px, pz),
        mesh=mesh,
        in_specs=(spec,) * 5,
        out_specs=(spec, spec),
        check_vma=False,
    )
```
